512 devices in a mesh: dp: 16 (over x, z_hi), seq: 32 (over y, z_lo, core).
Axes of the slice: x: 4, y: 4, z: 16 (z_hi: 4, z_lo: 4; z = z_hi * 4 + z_lo), core: 2. Of those that a mesh axis runs over, the one named last changes fastest.
Arguments:
- attention_queries: bfloat16 [16, 32, 128, 1536], P('dp', 'seq'), may hold values from -40 to 40
- attention_keys: bfloat16 [16, 32, 128, 1536], P('dp', 'seq'), may hold values from -40 to 40
- attention_values: bfloat16 [16, 32, 128, 1536], P('dp', 'seq'), may hold values from -6 to 6
- cotangent: bfloat16 [16, 32, 128, 1536], P('dp', 'seq'), may hold values from -1.5 to 1.5
- frozen_output_weight: bfloat16 [2, 1536, 1536], P(None, 'dp'), may hold values from -0.15625 to 0.15625
- adapter_down_factor: bfloat16 [2, 1536, 64], P(None, 'dp'), may hold values from -0.15625 to 0.15625
- adapter_up_factor: bfloat16 [2, 64, 1536], P(None, None, 'dp'), may hold values from -0.75 to 0.75
Outputs:
- blended: bfloat16 [16, 32, 128, 1536], P('dp', 'seq')
- grad_query: bfloat16 [16, 32, 128, 1536], P('dp', 'seq')
- grad_key: bfloat16 [16, 32, 128, 1536], P('dp', 'seq')
- grad_value: bfloat16 [16, 32, 128, 1536], P('dp', 'seq')
- grad_down: float32 [2, 1536, 64], P(None, 'dp')
- grad_up: float32 [2, 64, 1536], P(None, None, 'dp')
The draws below stay inside these ranges and needn't reach their ends.
All inputs are finite; a program needn't handle non-finite values.
Results may differ from the reference program's by a relative error of at most 0.029.
Values may be sent and summed in bfloat16 or wider, within the bound.
No kernel may reach another device: no remote copies, remote signals or barrier semaphores. Data moves between devices by JAX's collectives and lax.ppermute only.
A program may use at most 128 MiB of HBM per device.

```python
import jax
import jax.numpy as jnp
from jax import lax

CHANNEL_SLICE = 1536
HEADS = 12
HDIM = 128
ADAPTER_RANK = 64
PATCHES = 128
HEAD_FEATURES = 1536
FRAMES = 32
CLIPS = 16


def draw_attention_queries(key, part):
    key = jax.random.fold_in(key, 11)
    first = jax.random.fold_in(key, 0)
    shape = (CLIPS, FRAMES, PATCHES, HEADS * HDIM)
    sample = jnp.clip(jax.random.normal(first, shape, jnp.float32), -6.0, 6.0)
    return jnp.clip(sample, -40.0, 40.0).astype(jnp.bfloat16)


def draw_attention_keys(key, part):
    key = jax.random.fold_in(key, 23)
    first = jax.random.fold_in(key, 0)
    shape = (CLIPS, FRAMES, PATCHES, HEADS * HDIM)
    sample = jnp.clip(jax.random.normal(first, shape, jnp.float32), -6.0, 6.0)
    return jnp.clip(sample, -40.0, 40.0).astype(jnp.bfloat16)


def steps_of(rng, extent, cuts, low, largest):
    def one(position, blocks):
        draws = jax.random.uniform(jax.random.fold_in(jax.random.fold_in(rng, 6), position), (blocks,), jnp.float32, low / len(cuts), largest / len(cuts))
        return jnp.repeat(jnp.exp(draws), extent[position] // blocks).reshape((-1,) + (1,) * (len(extent) - position - 1))

    level = one(*cuts[0])
    for cut in cuts[1:]:
        level = level * one(*cut)
    return level


def normal_values(stream_key, extent, deviation, most, cuts=(), held_as=jnp.bfloat16):
    result = jax.random.normal(stream_key, extent, jnp.float32) * deviation
    if len(cuts) > 0:
        result = steps_of(stream_key, extent, cuts, -0.22, 0.18) * result
    return jnp.clip(result, min=-most, max=most).astype(held_as)


def setup_inputs(seed: int = 0) -> dict:
    key_list = jax.random.split(jax.random.key(seed), 8)
    return {
        "attention_queries": draw_attention_queries(jax.random.fold_in(key_list[7], 71), 0),
        "attention_keys": draw_attention_keys(jax.random.fold_in(key_list[7], 71), 0),
        "attention_values": normal_values(key_list[2], (CLIPS, FRAMES, PATCHES, HEAD_FEATURES), 1.0, 6.0, ((0, 16), (1, 32))),
        "cotangent": normal_values(key_list[3], (CLIPS, FRAMES, PATCHES, CHANNEL_SLICE), 0.25, 1.5, ((0, 16), (1, 32))),
        "frozen_output_weight": normal_values(key_list[4], (2, HEAD_FEATURES, CHANNEL_SLICE), HEAD_FEATURES ** -0.5, 0.15625, ((1, 16),)),
        "adapter_down_factor": normal_values(key_list[5], (2, HEAD_FEATURES, ADAPTER_RANK), HEAD_FEATURES ** -0.5, 0.15625, ((1, 16),)),
        "adapter_up_factor": normal_values(key_list[6], (2, ADAPTER_RANK, CHANNEL_SLICE), ADAPTER_RANK ** -0.5, 0.75, ((2, 16),)),
    }


adapter_gain = 2.0


def attend(query_heads, key_heads, value_heads):
    scale_factor = HDIM ** -0.5
    scores = jnp.einsum('blhe,bmhe->bhlm', query_heads.astype(jnp.float32), key_heads.astype(jnp.float32)) * scale_factor
    attention = jax.nn.softmax(scores, axis=-1)
    rounded = lax.optimization_barrier(attention.astype(jnp.bfloat16)).astype(jnp.float32)
    blended = jnp.einsum('bhlm,bmhe->blhe', rounded, value_heads.astype(jnp.float32))
    return attention, blended.astype(jnp.bfloat16)


def attend_back(query_heads, key_heads, value_heads, attention, upstream):
    scale_factor = HDIM ** -0.5
    rounded = lax.optimization_barrier(attention.astype(jnp.bfloat16)).astype(jnp.float32)
    upstream_wide = upstream.astype(jnp.float32)
    grad_value = jnp.einsum('bhlm,blhe->bmhe', rounded, upstream_wide)
    grad_attention = jnp.einsum('blhe,bmhe->bhlm', upstream_wide, value_heads.astype(jnp.float32))
    centre = jnp.sum(attention * grad_attention, axis=-1, keepdims=True)
    grad_scores = attention * (grad_attention - centre) * scale_factor
    grad_scores = lax.optimization_barrier(grad_scores.astype(jnp.bfloat16)).astype(jnp.float32)
    grad_query = jnp.einsum('bhlm,bmhe->blhe', grad_scores, key_heads.astype(jnp.float32))
    grad_key = jnp.einsum('bhlm,blhe->bmhe', grad_scores, query_heads.astype(jnp.float32))
    return grad_query, grad_key, grad_value


def swap_axes(tensor):
    return jnp.transpose(tensor, (1, 0, 2, 3))


def reference(attention_queries, attention_keys, attention_values, cotangent, frozen_output_weight, adapter_down_factor, adapter_up_factor):
    def one_clip(inputs):
        query_rows, key_rows, value_rows, upstream = inputs
        frame_count, patch_count = query_rows.shape[0], query_rows.shape[1]
        head_count = query_rows.shape[2] // HDIM
        row_count = frame_count * patch_count

        def to_heads(tensor):
            return tensor.reshape(frame_count, patch_count, head_count, HDIM)

        query_heads, key_heads, value_heads = to_heads(query_rows), to_heads(key_rows), to_heads(value_rows)
        spatial_probs, spatial_out = attend(query_heads, key_heads, value_heads)
        time_query, time_key, time_value = swap_axes(query_heads), swap_axes(key_heads), swap_axes(value_heads)
        temporal_probs, temporal_out = attend(time_query, time_key, time_value)
        attention_branches = (spatial_out.reshape(row_count, -1), swap_axes(temporal_out).reshape(row_count, -1))
        flattened_upstream = upstream.reshape(row_count, -1)
        summed_total = jnp.zeros((row_count, flattened_upstream.shape[1]), jnp.float32)
        down_factor_gradients, up_factor_gradients, upstreams = [], [], []
        for branch_member in range(2):
            reduced_rank_product = jnp.dot(attention_branches[branch_member], adapter_down_factor[branch_member], preferred_element_type=jnp.float32).astype(jnp.bfloat16)
            summed_total = summed_total + jnp.dot(attention_branches[branch_member], frozen_output_weight[branch_member], preferred_element_type=jnp.float32) + adapter_gain * jnp.dot(reduced_rank_product, adapter_up_factor[branch_member], preferred_element_type=jnp.float32)
            backward_rank = jnp.dot(flattened_upstream, adapter_up_factor[branch_member].T, preferred_element_type=jnp.float32).astype(jnp.bfloat16)
            branch_gradient = jnp.dot(flattened_upstream, frozen_output_weight[branch_member].T, preferred_element_type=jnp.float32) + adapter_gain * jnp.dot(backward_rank, adapter_down_factor[branch_member].T, preferred_element_type=jnp.float32)
            upstreams.append(branch_gradient.astype(jnp.bfloat16))
            up_factor_gradients.append(adapter_gain * jnp.dot(reduced_rank_product.T, flattened_upstream, preferred_element_type=jnp.float32))
            down_factor_gradients.append(adapter_gain * jnp.dot(attention_branches[branch_member].T, backward_rank, preferred_element_type=jnp.float32))
        blended = summed_total.astype(jnp.bfloat16).reshape(frame_count, patch_count, -1)
        space_grads = attend_back(query_heads, key_heads, value_heads, spatial_probs, to_heads(upstreams[0]))
        time_grads = attend_back(time_query, time_key, time_value, temporal_probs, swap_axes(to_heads(upstreams[1])))

        def combine(space, time_part):
            sent = lax.optimization_barrier(time_part.astype(jnp.bfloat16)).astype(jnp.float32)
            return (space + swap_axes(sent)).astype(jnp.bfloat16).reshape(frame_count, patch_count, -1)

        return (blended, combine(space_grads[0], time_grads[0]), combine(space_grads[1], time_grads[1]), combine(space_grads[2], time_grads[2]), jnp.stack(down_factor_gradients), jnp.stack(up_factor_gradients))

    results = lax.map(one_clip, (attention_queries, attention_keys, attention_values, cotangent))
    return (results[0], results[1], results[2], results[3], jnp.sum(results[4], axis=0), jnp.sum(results[5], axis=0))
```

```python
import functools

import jax
import jax.numpy as jnp
from jax import lax
from jax.experimental import pallas as pl
from jax.experimental.pallas import tpu as pltpu
from jax.sharding import Mesh
from jax.sharding import PartitionSpec as P

HDIM = 128
HEADS = 12
FEATURES = 1536
ROWS = 128
RANK = 64
GAIN = 2.0
SCALE = HDIM ** (-0.5)

AXES = ("x", "zh", "y", "zl", "c")
SIZES = (4, 4, 4, 4, 2)
SEQ = ("y", "zl", "c")
F32 = jnp.float32
BF16 = jnp.bfloat16
VMEM_LIMIT = 40 * 1024 * 1024


def nn(a, b):
    return lax.dot_general(a, b, (((1,), (0,)), ((), ())), preferred_element_type=F32)


def nt(a, b):
    return lax.dot_general(a, b, (((1,), (1,)), ((), ())), preferred_element_type=F32)


def tn(a, b):
    return lax.dot_general(a, b, (((0,), (0,)), ((), ())), preferred_element_type=F32)


def call(kernel, out_shape, in_specs, scratch, flops, nbytes):
    vmem = pl.BlockSpec(memory_space=pltpu.VMEM)
    return pl.pallas_call(
        kernel,
        out_shape=out_shape,
        in_specs=in_specs,
        out_specs=jax.tree.map(lambda _: vmem, out_shape),
        scratch_shapes=scratch,
        compiler_params=pltpu.CompilerParams(vmem_limit_bytes=VMEM_LIMIT),
        cost_estimate=pl.CostEstimate(flops=flops, bytes_accessed=nbytes, transcendentals=0),
    )


VM = pl.BlockSpec(memory_space=pltpu.VMEM)
ANY = pl.BlockSpec(memory_space=pl.ANY)
SM = pl.BlockSpec(memory_space=pltpu.SMEM)


def same_patch():
    rows = lax.broadcasted_iota(jnp.int32, (ROWS, ROWS), 0)
    columns = lax.broadcasted_iota(jnp.int32, (ROWS, ROWS), 1)
    return (rows % 4) == (columns % 4)


def forward_heads(q, k, v, probs_ref, out_ref, mask):
    for h in range(HEADS):
        scores = nt(q(h), k(h)) * SCALE
        if mask is not None:
            scores = jnp.where(mask, scores, -1e30)
        scores = jnp.exp(scores - jnp.max(scores, axis=-1, keepdims=True))
        probs = scores / jnp.sum(scores, axis=-1, keepdims=True)
        probs_ref[h] = probs
        out_ref[:, h * HDIM : (h + 1) * HDIM] = nn(probs.astype(BF16), v(h)).astype(BF16)


def backward_head(q, k, v, probs, up):
    value_term = tn(probs.astype(BF16), up)
    prob_term = nt(up, v)
    centre = jnp.sum(probs * prob_term, axis=-1, keepdims=True)
    score_term = (probs * (prob_term - centre) * SCALE).astype(BF16)
    return nn(score_term, k), tn(score_term, q), value_term


def head(ref, base=0):
    return lambda h: ref[:, base + h * HDIM : base + (h + 1) * HDIM]


def spatial_forward(q, k, v, probs_ref, out_ref):
    forward_heads(head(q), head(k), head(v), probs_ref, out_ref, None)


def temporal_forward(t, probs_ref, out_ref):
    forward_heads(head(t), head(t, FEATURES), head(t, 2 * FEATURES), probs_ref, out_ref, same_patch())


def adapters_kernel(place, pieces, o0, o1, cot, t, du_ref, rank0, rank1, grads, held, sems):
    x = place[0]
    copies = []
    for k in range(4):
        at = pl.multiple_of(((x - k) & 3) * 4, 4)
        for b in range(2):
            for half in range(2):
                copies.append(
                    pltpu.make_async_copy(
                        pieces.at[k, b, :, :, half * 128 : half * 128 + 128],
                        held.at[b, pl.ds(at, 4), half],
                        sems.at[len(copies)],
                    )
                )
    for copy in copies:
        copy.start()
    for copy in copies:
        copy.wait()
    lanes = lax.broadcasted_iota(jnp.int32, (ROWS, 128), 1) < RANK
    wide = lax.broadcasted_iota(jnp.int32, (FEATURES, 128), 1) < RANK
    for b in range(2):
        du = held[b].reshape(FEATURES, 128)
        du_ref[b] = du
        out = (o0, o1)[b][...]
        cotangent = cot[...] if b == 0 else t[:, 3 * FEATURES :]
        low = nn(out, du)
        back = nn(cotangent, du)
        low_back = jnp.where(lanes, low, back).astype(BF16)
        (rank0, rank1)[b][...] = low_back
        from_out = tn(out, low_back)
        from_cotangent = tn(cotangent, low_back)
        grads[b] = (GAIN * jnp.where(wide, from_cotangent, from_out)).astype(BF16)


def load_weight(place, mine, other, weight, sems):
    x, y, c = place[0], place[1], place[2]
    copies = []
    for side, arrays in ((c, mine), (1 - c, other)):
        for m in range(4):
            for k in range(4):
                row = jnp.where(side == 0, x - k, x - m) & 3
                column = jnp.where(side == 0, y - m, y - k) & 3
                copies.append(
                    pltpu.make_async_copy(
                        arrays[m].at[k],
                        weight.at[pl.ds(row * 4, 4), side, :, pl.ds(pl.multiple_of(column * 384, 128), 384)],
                        sems.at[len(copies)],
                    )
                )
    for copy in copies:
        copy.start()
    for copy in copies:
        copy.wait()


BLOCK = 256


def project(out, cotangent, low_back, du, weight, blended_ref, up_ref):
    zero = jnp.zeros((), BF16)

    def step(i, _):
        at = pl.multiple_of(i * BLOCK, BLOCK)
        here = du[pl.ds(at, BLOCK), :]
        low_back_value = low_back[...]
        is_down = lax.broadcasted_iota(jnp.int32, (BLOCK, 128), 1) < RANK
        down = jnp.where(is_down, here, zero)
        upper = jnp.where(is_down, zero, here)
        swapped = jnp.concatenate([low_back_value[:, RANK:], low_back_value[:, :RANK]], axis=1)
        rows = weight[pl.ds(at, BLOCK), :]
        columns = weight[:, pl.ds(at, BLOCK)]
        up = nt(cotangent(), rows) + GAIN * nt(swapped, down)
        blended = nn(out(), columns) + GAIN * nt(swapped, upper)
        up_ref[:, pl.ds(at, BLOCK)] = up.astype(up_ref.dtype)
        blended_ref[:, pl.ds(at, BLOCK)] = blended.astype(blended_ref.dtype)
        return 0

    lax.fori_loop(0, FEATURES // BLOCK, step, 0)


def temporal_project(place, m0, m1, m2, m3, p0, p1, p2, p3, o1, t, rank1, du, blended_ref, up_ref, weight, sems):
    load_weight(place, (m0, m1, m2, m3), (p0, p1, p2, p3), weight, sems)
    whole = weight.reshape(FEATURES, FEATURES)
    project(lambda: o1[...], lambda: t[:, 3 * FEATURES :], rank1, du.at[1], whole, blended_ref, up_ref)


def temporal_backward(t, probs, up, sent):
    for h in range(HEADS):
        terms = backward_head(
            head(t)(h), head(t, FEATURES)(h), head(t, 2 * FEATURES)(h), probs[h], head(up)(h)
        )
        for i, term in enumerate(terms):
            at = i * FEATURES + h * HDIM
            sent[:, at : at + HDIM] = term.astype(BF16)


def spatial_rest(
    place, m0, m1, m2, m3, p0, p1, p2, p3, o0, cot, rank0, du, q, k, v, probs, blended_ref, dq, dk, dv, up, weight, sems
):
    load_weight(place, (m0, m1, m2, m3), (p0, p1, p2, p3), weight, sems)
    whole = weight.reshape(FEATURES, FEATURES)
    project(lambda: o0[...], lambda: cot[...], rank0, du.at[0], whole, blended_ref, up)
    for h in range(HEADS):
        terms = backward_head(head(q)(h), head(k)(h), head(v)(h), probs[h], head(up)(h))
        for ref, term in zip((dq, dk, dv), terms):
            ref[:, h * HDIM : (h + 1) * HDIM] = term


def shape(dims, dtype=BF16):
    return jax.ShapeDtypeStruct(dims, dtype)


def index_of(x, zh, y, zl, c):
    return (((x * 4 + zh) * 4 + y) * 4 + zl) * 2 + c


def everywhere():
    for x in range(4):
        for zh in range(4):
            for y in range(4):
                for zl in range(4):
                    for c in range(2):
                        yield x, zh, y, zl, c


def permute(value, move):
    pairs = []
    for at in everywhere():
        to = move(*at)
        if to is not None:
            pairs.append((index_of(*at), index_of(*to)))
    return lax.ppermute(value, AXES, pairs)


def along_zh(step):
    return lambda x, zh, y, zl, c: (x, (zh + step) % 4, y, zl, c)


def along_first(step):
    return lambda x, zh, y, zl, c: ((x + step) % 4, zh, y, zl, c) if c == 0 else (x, zh, (y + step) % 4, zl, c)


def along_second(step):
    return lambda x, zh, y, zl, c: (x, zh, (y + step) % 4, zl, c) if c == 0 else ((x + step) % 4, zh, y, zl, c)


def other_core(x, zh, y, zl, c):
    return (x, zh, y, zl, 1 - c)


def first_to_second(x, zh, y, zl, c):
    return (x, zh, y, zl, 1) if c == 0 else None


def exchange(value, axes):
    return lax.all_to_all(value, axes, split_axis=0, concat_axis=0, tiled=True)


def local(q, k, v, cot, weight, down, up):
    out_dims = q.shape
    x, zh, y, c = (lax.axis_index(n) for n in ("x", "zh", "y", "c"))
    place = jnp.stack([x, y, c, zh]).astype(jnp.int32)
    q, k, v, cot = (a.reshape(ROWS, FEATURES) for a in (q, k, v, cot))

    piece = lax.dynamic_slice(weight, (0, c * 48, y * 384), (2, 48, 384))
    adapters = jnp.concatenate([down, jnp.swapaxes(up, 1, 2)], axis=2)
    adapters = jnp.concatenate([adapters[:, :48], adapters[:, 48:]], axis=2)
    first = jnp.concatenate([piece, adapters], axis=2)
    arrived = [permute(first, along_zh(s)) for s in (1, 2, 3)]
    turned = jnp.stack([arrived[2], arrived[1], arrived[0], first] * 2, axis=1)
    by_zh = lax.dynamic_slice(turned, (0, 3 - zh, 0, 0), (2, 4, 48, 640))

    t = exchange(jnp.concatenate([q, k, v, cot], axis=1).reshape(32, 4, 4 * FEATURES), SEQ)
    t = t.reshape(ROWS, 4 * FEATURES)

    probs0, o0 = call(
        spatial_forward, (shape((HEADS, ROWS, ROWS), F32), shape((ROWS, FEATURES))), [VM] * 3, [], 10**8, 10**7
    )(q, k, v)

    stage = [by_zh] + [permute(by_zh, along_first(s)) for s in (1, 2, 3)]
    adapter_pieces = jnp.stack([s[..., 384:] for s in stage])
    from_first = permute(adapter_pieces, first_to_second)
    adapter_pieces = jnp.where(c == 0, adapter_pieces, from_first)

    def rest_of_gather(b):
        held = jnp.stack([s[b, :, :, :384] for s in stage])
        mine = [held] + [permute(held, along_second(s)) for s in (1, 2, 3)]
        other = [permute(m, other_core) for m in mine]
        return mine + other

    weight1 = rest_of_gather(1)
    weight0 = rest_of_gather(0)

    probs1, o1 = call(
        temporal_forward, (shape((HEADS, ROWS, ROWS), F32), shape((ROWS, FEATURES))), [VM], [], 10**8, 10**7
    )(t)

    du, rank0, rank1, grads = call(
        adapters_kernel,
        (shape((2, FEATURES, 128)), shape((ROWS, 128)), shape((ROWS, 128)), shape((2, FEATURES, 128))),
        [SM, ANY] + [VM] * 4,
        [pltpu.VMEM((2, 16, 2, 48, 128), BF16), pltpu.SemaphoreType.DMA((16,))],
        10**8,
        10**7,
    )(place, adapter_pieces, o0, o1, cot, t)

    weight_scratch = [pltpu.VMEM((16, 2, 48, FEATURES), BF16), pltpu.SemaphoreType.DMA((32,))]
    blended1, up1 = call(
        temporal_project,
        (shape((ROWS, FEATURES)), shape((ROWS, FEATURES))),
        [SM] + [ANY] * 8 + [VM] * 4,
        weight_scratch,
        12 * 10**8,
        10**7,
    )(place, *weight1, o1, t, rank1, du)
    blended1 = exchange(blended1.reshape(32, 4, FEATURES), SEQ).reshape(ROWS, FEATURES)

    sent = call(temporal_backward, shape((ROWS, 3 * FEATURES)), [VM] * 3, [], 2 * 10**8, 10**7)(t, probs1, up1)
    returned = exchange(sent.reshape(32, 4, 3 * FEATURES), SEQ).reshape(ROWS, 3 * FEATURES)

    blended0, dq, dk, dv = call(
        spatial_rest,
        (shape((ROWS, FEATURES), F32),) * 4,
        [SM] + [ANY] * 8 + [VM] * 8,
        [pltpu.VMEM((ROWS, FEATURES), BF16)] + weight_scratch,
        14 * 10**8,
        2 * 10**7,
    )(place, *weight0, o0, cot, rank0, du, q, k, v, probs0)

    summed = grads.reshape(2, 16, 4, 24, 128).transpose(2, 0, 1, 3, 4).reshape(8, 16 * 24, 128)
    summed = exchange(summed, ("y", "c")).astype(F32).sum(0).astype(BF16)
    summed = exchange(summed.reshape(4, 96, 128), "x").astype(F32).sum(0).astype(BF16)
    summed = jnp.broadcast_to(summed.reshape(4, 1, 24, 128), (4, 4, 24, 128)).reshape(16, 24, 128)
    summed = exchange(summed, ("zh", "zl")).astype(F32).sum(0).astype(BF16)
    summed = exchange(jnp.broadcast_to(summed[None], (8, 24, 128)), ("y", "c"))
    summed = summed.reshape(4, 2, 24, 128).transpose(1, 0, 2, 3).reshape(2, 96, 128).astype(F32)
    grad_up = jnp.swapaxes(summed[:, :, :RANK], 1, 2)
    grad_down = summed[:, :, RANK:]

    def combine(mine, arrived):
        return (mine + arrived.astype(F32)).astype(BF16).reshape(out_dims)

    return (
        combine(blended0, blended1),
        combine(dq, returned[:, :FEATURES]),
        combine(dk, returned[:, FEATURES : 2 * FEATURES]),
        combine(dv, returned[:, 2 * FEATURES :]),
        grad_down,
        grad_up,
    )


def solution(mesh):
    fine = Mesh(mesh.devices.reshape(SIZES), AXES)
    dp, seq = ("x", "zh"), SEQ
    tokens = P(dp, seq, None, None)
    rows, columns = P(None, dp, None), P(None, None, dp)
    return jax.shard_map(
        local,
        mesh=fine,
        in_specs=(tokens,) * 4 + (rows, rows, columns),
        out_specs=(tokens,) * 4 + (rows, columns),
        check_vma=False,
    )
```

```python
import jax
import jax.numpy as jnp
from jax import lax
from jax.experimental import pallas as pl
from jax.experimental.pallas import tpu as pltpu
from jax.sharding import Mesh
from jax.sharding import PartitionSpec as P

HDIM = 128
HEADS = 12
FEATURES = 1536
ROWS = 128
BOTH = 2 * ROWS
RANK = 64
GAIN = 2.0
SCALE = HDIM ** (-0.5)
WIDE = 4 * FEATURES
COT = 3 * FEATURES
SLICE = 384
BLOCK = 256

AXES = ("x", "zh", "y", "zl", "c")
SIZES = (4, 4, 4, 4, 2)
F32 = jnp.float32
BF16 = jnp.bfloat16

VM = pl.BlockSpec(memory_space=pltpu.VMEM)
ANY = pl.BlockSpec(memory_space=pl.ANY)
SM = pl.BlockSpec(memory_space=pltpu.SMEM)


def nn(a, b):
    return lax.dot_general(a, b, (((1,), (0,)), ((), ())), preferred_element_type=F32)


def nt(a, b):
    return lax.dot_general(a, b, (((1,), (1,)), ((), ())), preferred_element_type=F32)


def tn(a, b):
    return lax.dot_general(a, b, (((0,), (0,)), ((), ())), preferred_element_type=F32)


def shape(dims, dtype=BF16):
    return jax.ShapeDtypeStruct(dims, dtype)


def call(kernel, out_shape, in_specs, out_specs, scratch, flops, nbytes, vmem_mib=8):
    return pl.pallas_call(
        kernel,
        out_shape=out_shape,
        in_specs=in_specs,
        out_specs=out_specs,
        scratch_shapes=scratch,
        compiler_params=pltpu.CompilerParams(vmem_limit_bytes=vmem_mib * 2**20),
        cost_estimate=pl.CostEstimate(flops=flops, bytes_accessed=nbytes, transcendentals=0),
    )


def head(ref, h, base=0):
    return ref[:, base + h * HDIM : base + (h + 1) * HDIM]


def place_zh(place, s0, s1, s2, s3, held):
    for k, ref in enumerate((s0, s1, s2, s3)):
        held[(place[2] - k) & 3] = ref[...]


def wait_all(copies):
    for copy in copies:
        copy.wait()


def start_rows(place, own_time, own_space, got, rows, sems):
    @pl.when(place[3] == 0)
    def _():
        pltpu.make_async_copy(own_time, rows.at[0:ROWS], sems.at[0]).start()

    @pl.when(place[3] != 0)
    def _():
        pltpu.make_async_copy(own_space, rows.at[0:ROWS], sems.at[0]).start()

    copies = [
        pltpu.make_async_copy(own_time, rows.at[0:ROWS], sems.at[0]),
        pltpu.make_async_copy(got, rows.at[ROWS:BOTH], sems.at[1]),
    ]
    copies[1].start()
    return copies


def forward(place, own_time, own_space, got, probs_out, out, rows, probs, sems):
    wait_all(start_rows(place, own_time, own_space, got, rows, sems))
    time = place[3] == 0
    across = lax.broadcasted_iota(jnp.int32, (BOTH, BOTH), 0)
    along = lax.broadcasted_iota(jnp.int32, (BOTH, BOTH), 1)
    mask = jnp.where(time, across & 7, across >> 7) == jnp.where(time, along & 7, along >> 7)
    copies = []
    for h in range(HEADS):
        scores = nt(head(rows, h), head(rows, h, FEATURES)) * SCALE
        scores = jnp.where(mask, scores, -1e30)
        scores = jnp.exp(scores - jnp.max(scores, axis=-1, keepdims=True))
        value = scores / jnp.sum(scores, axis=-1, keepdims=True)
        probs[h] = value
        copies.append(pltpu.make_async_copy(probs.at[h], probs_out.at[h], sems.at[2 + h]))
        copies[-1].start()
        out[:, h * HDIM : (h + 1) * HDIM] = nn(value.astype(BF16), head(rows, h, 2 * FEATURES)).astype(BF16)
    wait_all(copies)


def adapters_kernel(place, m0, m1, m2, m3, own_time, own_space, got, out, du_out, low_back_out, grads, rows, du, sems):
    arrays = (m0, m1, m2, m3)
    x, y, c = place[0], place[1], place[3]

    def pieces(first_is_x):
        made = []
        for across in range(4):
            for down in (0, 2):
                second, first = (down, across) if first_is_x else (across, down)
                half = ((y - down) & 3) >> 1
                for part in range(3):
                    made.append(
                        pltpu.make_async_copy(
                            arrays[second].at[first, :, 96:112, part * 128 : part * 128 + 128],
                            du.at[pl.ds(((x - across) & 3) * 4, 4), pl.ds(pl.multiple_of(48 * half + 16 * part, 16), 16)],
                            sems.at[2 + len(made)],
                        )
                    )
        return made

    @pl.when(c == 0)
    def _():
        for copy in pieces(True):
            copy.start()

    @pl.when(c != 0)
    def _():
        for copy in pieces(False):
            copy.start()

    others = start_rows(
        place, own_time.at[:, COT:], own_space.at[:, COT:], got.at[:, COT:], rows, sems
    )
    wait_all(others)
    wait_all(pieces(True))
    factors = du[...].reshape(FEATURES, 128)
    du_out[...] = factors
    left = lax.broadcasted_iota(jnp.int32, (BOTH, 128), 1) < RANK
    low_back = jnp.where(left, nn(out[...], factors), nn(rows[...], factors)).astype(BF16)
    low_back_out[...] = low_back
    left = lax.broadcasted_iota(jnp.int32, (FEATURES, 128), 1) < RANK
    grads[...] = (GAIN * jnp.where(left, tn(rows[...], low_back), tn(out[...], low_back))).astype(BF16)


def rest(
    place, m0, m1, m2, m3, own_time, own_space, got, probs_in, out, low_back, du,
    here_out, there_out, weight, rows, probs, up, sent, sems, weight_sems,
):
    arrays = (m0, m1, m2, m3)
    x, y, c = place[0], place[1], place[3]
    copies = []
    for second in range(4):
        for first in range(4):
            row = jnp.where(c == 0, x - first, x - second) & 3
            column = jnp.where(c == 0, y - second, y - first) & 3
            copies.append(
                pltpu.make_async_copy(
                    arrays[second].at[first, :, 0:96, :],
                    weight.at[pl.ds(row * 4, 4), :, pl.ds(pl.multiple_of(column * SLICE, 128), SLICE)],
                    weight_sems.at[len(copies)],
                )
            )
            copies[-1].start()
    copies += start_rows(place, own_time, own_space, got, rows, sems)
    probs_copy = pltpu.make_async_copy(probs_in, probs, sems.at[2])
    probs_copy.start()
    wait_all(copies)
    whole = weight.reshape(FEATURES, FEATURES)
    zero = jnp.zeros((), BF16)

    def project(i, _):
        at = pl.multiple_of(i * BLOCK, BLOCK)
        factors = du[pl.ds(at, BLOCK), :]
        is_down = lax.broadcasted_iota(jnp.int32, (BLOCK, 128), 1) < RANK
        down = jnp.where(is_down, factors, zero)
        upper = jnp.where(is_down, zero, factors)
        swapped = jnp.concatenate([low_back[:, RANK:], low_back[:, :RANK]], axis=1)
        upstream = nt(rows[:, COT:], whole[pl.ds(at, BLOCK), :]) + GAIN * nt(swapped, down)
        up[:, pl.ds(at, BLOCK)] = upstream.astype(BF16)
        blended = nn(out[...], whole[:, pl.ds(at, BLOCK)]) + GAIN * nt(swapped, upper)
        sent[:, pl.ds(pl.multiple_of(COT + at, BLOCK), BLOCK)] = blended.astype(BF16)
        return 0

    lax.fori_loop(0, FEATURES // BLOCK, project, 0)
    probs_copy.wait()
    for h in range(HEADS):
        value = probs[h]
        upstream = head(up, h)
        value_term = tn(value.astype(BF16), upstream)
        prob_term = nt(upstream, head(rows, h, 2 * FEATURES))
        centre = jnp.sum(value * prob_term, axis=-1, keepdims=True)
        score_term = (value * (prob_term - centre) * SCALE).astype(BF16)
        terms = (nn(score_term, head(rows, h, FEATURES)), tn(score_term, head(rows, h)), value_term)
        for i, term in enumerate(terms):
            at = i * FEATURES + h * HDIM
            sent[:, at : at + HDIM] = term.astype(BF16)
    copies = [
        pltpu.make_async_copy(sent.at[0:ROWS], here_out, sems.at[3]),
        pltpu.make_async_copy(sent.at[ROWS:BOTH], there_out, sems.at[4]),
    ]
    for copy in copies:
        copy.start()
    wait_all(copies)


def index_of(x, zh, y, zl, c):
    return (((x * 4 + zh) * 4 + y) * 4 + zl) * 2 + c


def permute(value, move):
    pairs = []
    for x in range(4):
        for zh in range(4):
            for y in range(4):
                for zl in range(4):
                    for c in range(2):
                        pairs.append((index_of(x, zh, y, zl, c), index_of(*move(x, zh, y, zl, c))))
    return lax.ppermute(value, AXES, pairs)


def along_zh(step):
    return lambda x, zh, y, zl, c: (x, (zh + step) % 4, y, zl, c)


def along_first(step):
    return lambda x, zh, y, zl, c: ((x + step) % 4, zh, y, zl, c) if c == 0 else (x, zh, (y + step) % 4, zl, c)


def along_second(step):
    return lambda x, zh, y, zl, c: (x, zh, (y + step) % 4, zl, c) if c == 0 else ((x + step) % 4, zh, y, zl, c)


def other_core(x, zh, y, zl, c):
    return (x, zh, y, zl, 1 - c)


def exchange(value, axes):
    return lax.all_to_all(value, axes, split_axis=0, concat_axis=0, tiled=True)


def local(q, k, v, cot, weight, down, up):
    out_dims = q.shape
    x, zh, y, c = (lax.axis_index(n) for n in ("x", "zh", "y", "c"))
    place = jnp.stack([x, y, zh, c]).astype(jnp.int32)
    space = jnp.concatenate([a.reshape(ROWS, FEATURES) for a in (q, k, v, cot)], axis=1)

    branch = 1 - c
    piece = lax.dynamic_slice(weight, (branch, 0, y * SLICE), (1, 96, SLICE))[0]
    adapters = jnp.concatenate([down, jnp.swapaxes(up, 1, 2)], axis=2)
    adapters = lax.dynamic_slice(adapters, (branch, (y // 2) * 48, 0), (1, 48, 128))
    adapters = adapters.reshape(3, 16, 128).transpose(1, 0, 2).reshape(16, SLICE)
    first = jnp.concatenate([piece, adapters], axis=0)
    arrived = [permute(first, along_zh(s)) for s in (1, 2, 3)]
    held = call(place_zh, shape((4, 112, SLICE)), [SM] + [VM] * 4, VM, [], 10**6, 10**6)(place, first, *arrived)

    space, held = lax.optimization_barrier((space, held))
    time = exchange(space.reshape(16, 8, WIDE), ("y", "zl")).reshape(ROWS, WIDE)
    held = jnp.stack([held] + [permute(held, along_first(s)) for s in (1, 2, 3)])
    gathered = [held] + [permute(held, along_second(s)) for s in (1, 2, 3)]
    got = permute(jnp.where(c == 0, space, time), other_core)

    probs, out = call(
        forward,
        (shape((HEADS, BOTH, BOTH), F32), shape((BOTH, FEATURES))),
        [SM] + [ANY] * 3,
        (ANY, VM),
        [pltpu.VMEM((BOTH, WIDE), BF16), pltpu.VMEM((HEADS, BOTH, BOTH), F32), pltpu.SemaphoreType.DMA((14,))],
        4 * 10**8,
        10**7,
        16,
    )(place, time, space, got)

    du, low_back, grads = call(
        adapters_kernel,
        (shape((FEATURES, 128)), shape((BOTH, 128)), shape((FEATURES, 128))),
        [SM] + [ANY] * 7 + [VM],
        (VM, VM, VM),
        [pltpu.VMEM((BOTH, FEATURES), BF16), pltpu.VMEM((16, 96, 128), BF16), pltpu.SemaphoreType.DMA((26,))],
        4 * 10**8,
        5 * 10**6,
        16,
    )(place, *gathered, time, space, got, out)

    here, there = call(
        rest,
        (shape((ROWS, WIDE)), shape((ROWS, WIDE))),
        [SM] + [ANY] * 8 + [VM] * 3,
        (ANY, ANY),
        [
            pltpu.VMEM((16, 96, FEATURES), BF16),
            pltpu.VMEM((BOTH, WIDE), BF16),
            pltpu.VMEM((HEADS, BOTH, BOTH), F32),
            pltpu.VMEM((BOTH, FEATURES), BF16),
            pltpu.VMEM((BOTH, WIDE), BF16),
            pltpu.SemaphoreType.DMA((5,)),
            pltpu.SemaphoreType.DMA((16,)),
        ],
        3 * 10**9,
        2 * 10**7,
        32,
    )(place, *gathered, time, space, got, probs, out, low_back, du)

    summed = grads.reshape(16, 4, 24, 128).transpose(1, 0, 2, 3).reshape(4, 384, 128)
    summed = exchange(summed, "y").astype(F32).sum(0).astype(BF16)
    summed = exchange(summed.reshape(4, 96, 128), "x").astype(F32).sum(0).astype(BF16)

    other = permute(there, other_core)
    back = jnp.where(c == 0, here, other)
    back, summed = lax.optimization_barrier((back, summed))
    back = exchange(back.reshape(16, 8, WIDE), ("y", "zl")).reshape(ROWS, WIDE)

    summed = lax.psum(summed, "zh")
    summed = lax.dynamic_slice(summed, (zh * 24, 0), (24, 128))
    summed = lax.psum(summed, "zl")
    summed = lax.all_gather(summed, "y", tiled=True)
    pair = permute(summed, other_core)
    summed = jnp.stack([jnp.where(c == 0, pair, summed), jnp.where(c == 0, summed, pair)]).astype(F32)
    grad_up = jnp.swapaxes(summed[:, :, :RANK], 1, 2)
    grad_down = summed[:, :, RANK:]

    mine = jnp.where(c == 0, other, here)
    total = [
        (mine[:, at : at + FEATURES].astype(F32) + back[:, at : at + FEATURES].astype(F32)).astype(BF16).reshape(out_dims)
        for at in (COT, 0, FEATURES, 2 * FEATURES)
    ]
    return (*total, grad_down, grad_up)


def solution(mesh):
    fine = Mesh(mesh.devices.reshape(SIZES), AXES)
    dp, seq = ("x", "zh"), ("y", "zl", "c")
    tokens = P(dp, seq, None, None)
    rows, columns = P(None, dp, None), P(None, None, dp)
    return jax.shard_map(
        local,
        mesh=fine,
        in_specs=(tokens,) * 4 + (rows, rows, columns),
        out_specs=(tokens,) * 4 + (rows, columns),
        check_vma=False,
    )
```

```python
import jax
import jax.numpy as jnp
from jax import lax
from jax.experimental import pallas as pl
from jax.experimental.pallas import tpu as pltpu
from jax.sharding import Mesh
from jax.sharding import PartitionSpec as P

HDIM = 128
HEADS = 12
FEATURES = 1536
ROWS = 128
BOTH = 2 * ROWS
RANK = 64
GAIN = 2.0
SCALE = HDIM ** (-0.5)
WIDE = 4 * FEATURES
COT = 3 * FEATURES
SLICE = 384
BLOCK = 256
GROUP = 3

AXES = ("x", "zh", "y", "zl", "c")
SIZES = (4, 4, 4, 4, 2)
F32 = jnp.float32
BF16 = jnp.bfloat16

VM = pl.BlockSpec(memory_space=pltpu.VMEM)
HBM = pl.BlockSpec(memory_space=pltpu.HBM)
SM = pl.BlockSpec(memory_space=pltpu.SMEM)


def nn(a, b):
    return lax.dot_general(a, b, (((1,), (0,)), ((), ())), preferred_element_type=F32)


def nt(a, b):
    return lax.dot_general(a, b, (((1,), (1,)), ((), ())), preferred_element_type=F32)


def tn(a, b):
    return lax.dot_general(a, b, (((0,), (0,)), ((), ())), preferred_element_type=F32)


def shape(dims, dtype=BF16):
    return jax.ShapeDtypeStruct(dims, dtype)


def call(kernel, out_shape, in_specs, out_specs, scratch, flops, nbytes, vmem_mib=62):
    return pl.pallas_call(
        kernel,
        out_shape=out_shape,
        in_specs=in_specs,
        out_specs=out_specs,
        scratch_shapes=scratch,
        compiler_params=pltpu.CompilerParams(vmem_limit_bytes=vmem_mib * 2**20),
        cost_estimate=pl.CostEstimate(flops=flops, bytes_accessed=nbytes, transcendentals=0),
    )


def head(ref, h, base=0):
    return ref[:, base + h * HDIM : base + (h + 1) * HDIM]


def piece_of(arrays, second, first):
    return arrays[second][first // 2].at[first % 2]


def wait_all(copies):
    for copy in copies:
        copy.wait()


def start_rows(place, time, space, other_time, other_space, rows, sems, spans):
    def copies(own, other):
        return [
            (
                pltpu.make_async_copy(own.at[:, at:to], rows.at[0:ROWS, into : into + to - at], sems.at[2 * i]),
                pltpu.make_async_copy(other.at[:, at:to], rows.at[ROWS:BOTH, into : into + to - at], sems.at[2 * i + 1]),
            )
            for i, (at, to, into) in enumerate(spans)
        ]

    @pl.when(place[3] == 0)
    def _():
        for pair in copies(time, other_time):
            wait_none(pair)

    @pl.when(place[3] != 0)
    def _():
        for pair in copies(space, other_space):
            wait_none(pair)

    return copies(time, other_time)


def wait_none(copies):
    for copy in copies:
        copy.start()


def spans_of_heads():
    return [
        (part * FEATURES + at, part * FEATURES + at + GROUP * HDIM, part * FEATURES + at)
        for at in range(0, FEATURES, GROUP * HDIM)
        for part in range(3)
    ]


def forward(
    place, e0, l0, e1, l1, e2, l2, e3, l3, time, space, other_time, other_space,
    probs_out, out_out, du_out, low_back_out, grads_out, rows, probs, out, du, low_back, grads, sems, row_sems, du_sems,
):
    arrays = ((e0, l0), (e1, l1), (e2, l2), (e3, l3))
    x, y, c = place[0], place[1], place[3]

    def pieces(first_is_x):
        made = []
        for across in range(4):
            for steps in (0, 2):
                second, first = (steps, across) if first_is_x else (across, steps)
                half = ((y - steps) & 3) >> 1
                for part in range(3):
                    made.append(
                        pltpu.make_async_copy(
                            piece_of(arrays, second, first).at[:, 96:112, part * 128 : part * 128 + 128],
                            du.at[pl.ds(((x - across) & 3) * 4, 4), pl.ds(pl.multiple_of(48 * half + 16 * part, 16), 16)],
                            du_sems.at[len(made)],
                        )
                    )
        return made

    loads = start_rows(
        place, time, space, other_time, other_space, rows, row_sems, spans_of_heads() + [(COT, WIDE, COT)]
    )

    @pl.when(c == 0)
    def _():
        wait_none(pieces(True))

    @pl.when(c != 0)
    def _():
        wait_none(pieces(False))

    across = lax.broadcasted_iota(jnp.int32, (BOTH, BOTH), 0)
    along = lax.broadcasted_iota(jnp.int32, (BOTH, BOTH), 1)
    mask = jnp.where(c == 0, across & 7, across >> 7) == jnp.where(c == 0, along & 7, along >> 7)
    copies = []
    for h in range(HEADS):
        if h % GROUP == 0:
            for pair in loads[h // GROUP * 3 : h // GROUP * 3 + 3]:
                wait_all(pair)
        scores = nt(head(rows, h), head(rows, h, FEATURES)) * SCALE
        scores = jnp.where(mask, scores, -1e30)
        scores = jnp.exp(scores - jnp.max(scores, axis=-1, keepdims=True))
        value = scores / jnp.sum(scores, axis=-1, keepdims=True)
        probs[h] = value
        copies.append(pltpu.make_async_copy(probs.at[h], probs_out.at[h], sems.at[h]))
        copies[-1].start()
        out[:, h * HDIM : (h + 1) * HDIM] = nn(value.astype(BF16), head(rows, h, 2 * FEATURES)).astype(BF16)
    wait_all(pieces(True))
    wait_all(loads[-1])
    copies += [
        pltpu.make_async_copy(out, out_out, sems.at[HEADS]),
        pltpu.make_async_copy(du, du_out, sems.at[HEADS + 1]),
    ]
    wait_none(copies[-2:])
    factors = du[...].reshape(FEATURES, 128)
    left = lax.broadcasted_iota(jnp.int32, (BOTH, 128), 1) < RANK
    low_back[...] = jnp.where(left, nn(out[...], factors), nn(rows[:, COT:], factors)).astype(BF16)
    left = lax.broadcasted_iota(jnp.int32, (FEATURES, 128), 1) < RANK
    grads[...] = (GAIN * jnp.where(left, tn(rows[:, COT:], low_back[...]), tn(out[...], low_back[...]))).astype(BF16)
    copies += [
        pltpu.make_async_copy(low_back, low_back_out, sems.at[HEADS + 2]),
        pltpu.make_async_copy(grads, grads_out, sems.at[HEADS + 3]),
    ]
    wait_none(copies[-2:])
    wait_all(copies)


def project(
    place, e0, l0, e1, l1, e2, l2, e3, l3, time, space, other_time, other_space, out_in, low_back_in, du_in,
    up_out, blended_out, weight, rows, out, low_back, du, up, blended, sems, row_sems, weight_sems,
):
    x, y, c = place[0], place[1], place[3]
    copies = []
    for second in range(4):
        for first in range(4):
            row = jnp.where(c == 0, x - first, x - second) & 3
            column = jnp.where(c == 0, y - second, y - first) & 3
            copies.append(
                pltpu.make_async_copy(
                    piece_of(((e0, l0), (e1, l1), (e2, l2), (e3, l3)), second, first).at[:, 0:96, :],
                    weight.at[pl.ds(row * 4, 4), :, pl.ds(pl.multiple_of(column * SLICE, 128), SLICE)],
                    weight_sems.at[len(copies)],
                )
            )
            copies[-1].start()
    smaller = [
        pltpu.make_async_copy(source, target, sems.at[i])
        for i, (source, target) in enumerate(((out_in, out), (low_back_in, low_back), (du_in, du)))
    ]
    wait_none(smaller)
    loads = start_rows(place, time, space, other_time, other_space, rows, row_sems, [(COT, WIDE, 0)])
    wait_all(copies + smaller)
    wait_all(loads[0])
    whole = weight.reshape(FEATURES, FEATURES)
    factors_of = du.reshape(FEATURES, 128)
    zero = jnp.zeros((), BF16)

    def step(i, _):
        at = pl.multiple_of(i * BLOCK, BLOCK)
        factors = factors_of[pl.ds(at, BLOCK), :]
        is_down = lax.broadcasted_iota(jnp.int32, (BLOCK, 128), 1) < RANK
        down = jnp.where(is_down, factors, zero)
        upper = jnp.where(is_down, zero, factors)
        swapped = jnp.concatenate([low_back[:, RANK:], low_back[:, :RANK]], axis=1)
        upstream = nt(rows[...], whole[pl.ds(at, BLOCK), :]) + GAIN * nt(swapped, down)
        up[:, pl.ds(at, BLOCK)] = upstream.astype(BF16)
        total = nn(out[...], whole[:, pl.ds(at, BLOCK)]) + GAIN * nt(swapped, upper)
        blended[:, pl.ds(at, BLOCK)] = total.astype(BF16)
        return 0

    lax.fori_loop(0, FEATURES // BLOCK, step, 0)
    copies = [
        pltpu.make_async_copy(up, up_out, sems.at[3]),
        pltpu.make_async_copy(blended, blended_out, sems.at[4]),
    ]
    wait_none(copies)
    wait_all(copies)


def backward(
    place, time, space, other_time, other_space, probs_in, up_in, blended_in,
    here_out, there_out, rows, probs, up, sent, sems, row_sems, out_sems,
):
    load_up = pltpu.make_async_copy(up_in, up, sems.at[0])
    load_blended = pltpu.make_async_copy(blended_in, sent.at[:, COT:], sems.at[1])
    loads = [pltpu.make_async_copy(probs_in.at[h], probs.at[h], sems.at[2 + h]) for h in range(HEADS)]
    load_up.start()
    wait_none(loads[:GROUP])
    load_rows = start_rows(place, time, space, other_time, other_space, rows, row_sems, spans_of_heads())
    wait_none(loads[GROUP:])
    load_blended.start()
    load_up.wait()
    copies = []

    def send(at, to):
        for ref, here, there in ((here_out, 0, ROWS), (there_out, ROWS, BOTH)):
            copies.append(pltpu.make_async_copy(sent.at[here:there, at:to], ref.at[:, at:to], out_sems.at[len(copies)]))
            copies[-1].start()

    for h in range(HEADS):
        if h % GROUP == 0:
            for pair in load_rows[h // GROUP * 3 : h // GROUP * 3 + 3]:
                wait_all(pair)
        loads[h].wait()
        value = probs[h]
        upstream = head(up, h)
        value_term = tn(value.astype(BF16), upstream)
        prob_term = nt(upstream, head(rows, h, 2 * FEATURES))
        centre = jnp.sum(value * prob_term, axis=-1, keepdims=True)
        score_term = (value * (prob_term - centre) * SCALE).astype(BF16)
        terms = (nn(score_term, head(rows, h, FEATURES)), tn(score_term, head(rows, h)), value_term)
        for i, term in enumerate(terms):
            at = i * FEATURES + h * HDIM
            sent[:, at : at + HDIM] = term.astype(BF16)
        if h % GROUP == GROUP - 1:
            for at in range(0, COT, FEATURES):
                send(at + (h + 1 - GROUP) * HDIM, at + (h + 1) * HDIM)
    load_blended.wait()
    send(COT, WIDE)
    wait_all(copies)


def choose(place, on_first, on_second, out, sem):
    @pl.when(place[3] == 0)
    def _():
        pltpu.make_async_copy(on_first, out, sem.at[0]).start()

    @pl.when(place[3] != 0)
    def _():
        pltpu.make_async_copy(on_second, out, sem.at[0]).start()

    pltpu.make_async_copy(on_first, out, sem.at[0]).wait()


def index_of(x, zh, y, zl, c):
    return (((x * 4 + zh) * 4 + y) * 4 + zl) * 2 + c


def permute(value, move):
    pairs = []
    for x in range(4):
        for zh in range(4):
            for y in range(4):
                for zl in range(4):
                    for c in range(2):
                        to = move(x, zh, y, zl, c)
                        if to is not None:
                            pairs.append((index_of(x, zh, y, zl, c), index_of(*to)))
    return lax.ppermute(value, AXES, pairs)


def along_first(step):
    return lambda x, zh, y, zl, c: ((x + step) % 4, zh, y, zl, c) if c == 0 else (x, zh, (y + step) % 4, zl, c)


def along_second(step):
    return lambda x, zh, y, zl, c: (x, zh, (y + step) % 4, zl, c) if c == 0 else ((x + step) % 4, zh, y, zl, c)


def other_core(x, zh, y, zl, c):
    return (x, zh, y, zl, 1 - c)


def to_first_core(x, zh, y, zl, c):
    return (x, zh, y, zl, 0) if c == 1 else None


def to_second_core(x, zh, y, zl, c):
    return (x, zh, y, zl, 1) if c == 0 else None


def exchange(value, axes):
    return lax.all_to_all(value, axes, split_axis=0, concat_axis=0, tiled=True)


def local(q, k, v, cot, weight, down, up):
    out_dims = q.shape
    x, zh, y, c = (lax.axis_index(n) for n in ("x", "zh", "y", "c"))
    place = jnp.stack([x, y, zh, c]).astype(jnp.int32)
    space = jnp.concatenate([a.reshape(ROWS, FEATURES) for a in (q, k, v, cot)], axis=1)

    branch = 1 - c
    piece = lax.dynamic_slice(weight, (branch, 0, y * SLICE), (1, 96, SLICE))[0]
    adapters = jnp.concatenate([down, jnp.swapaxes(up, 1, 2)], axis=2)
    adapters = lax.dynamic_slice(adapters, (branch, (y // 2) * 48, 0), (1, 48, 128))
    adapters = adapters.reshape(3, 16, 128).transpose(1, 0, 2).reshape(16, SLICE)
    first = jnp.concatenate([piece, adapters], axis=0)
    held = lax.all_gather(first, "zh")

    other_space = permute(space, to_second_core)
    space, held = lax.optimization_barrier((space, held))
    arrived = [permute(held, along_first(s)) for s in (1, 2, 3)]
    time = exchange(space.reshape(16, 8, WIDE), ("y", "zl")).reshape(ROWS, WIDE)
    early, late = jnp.stack([held, arrived[0]]), jnp.stack(arrived[1:])
    early_below, late_above = permute(early, along_second(1)), permute(late, along_second(3))
    early_above, late_below = permute(early, along_second(3)), permute(late, along_second(1))
    early_far, late_far = permute(early_below, along_second(1)), permute(late_above, along_second(3))
    gathered = [early, late, early_below, late_below, early_far, late_far, early_above, late_above]
    time, other_space, *gathered = lax.optimization_barrier((time, other_space, *gathered))
    other_time = permute(time, to_first_core)
    tokens = (time, space, other_time, other_space)

    probs, out, du, low_back, grads = call(
        forward,
        (
            shape((HEADS, BOTH, BOTH), F32),
            shape((BOTH, FEATURES)),
            shape((16, 96, 128)),
            shape((BOTH, 128)),
            shape((FEATURES, 128)),
        ),
        [SM] + [HBM] * 12,
        (HBM,) * 5,
        [
            pltpu.VMEM((BOTH, WIDE), BF16),
            pltpu.VMEM((HEADS, BOTH, BOTH), F32),
            pltpu.VMEM((BOTH, FEATURES), BF16),
            pltpu.VMEM((16, 96, 128), BF16),
            pltpu.VMEM((BOTH, 128), BF16),
            pltpu.VMEM((FEATURES, 128), BF16),
            pltpu.SemaphoreType.DMA((16,)),
            pltpu.SemaphoreType.DMA((26,)),
            pltpu.SemaphoreType.DMA((24,)),
        ],
        8 * 10**8,
        10**7,
    )(place, *gathered, *tokens)

    summed = grads.reshape(4, 4, 4, 24, 128).transpose(0, 2, 1, 3, 4).reshape(16, 96, 128)
    summed = exchange(summed, ("x", "y"))

    up, blended = call(
        project,
        (shape((BOTH, FEATURES)), shape((BOTH, FEATURES))),
        [SM] + [HBM] * 15,
        (HBM, HBM),
        [
            pltpu.VMEM((16, 96, FEATURES), BF16),
            pltpu.VMEM((BOTH, FEATURES), BF16),
            pltpu.VMEM((BOTH, FEATURES), BF16),
            pltpu.VMEM((BOTH, 128), BF16),
            pltpu.VMEM((16, 96, 128), BF16),
            pltpu.VMEM((BOTH, FEATURES), BF16),
            pltpu.VMEM((BOTH, FEATURES), BF16),
            pltpu.SemaphoreType.DMA((5,)),
            pltpu.SemaphoreType.DMA((2,)),
            pltpu.SemaphoreType.DMA((16,)),
        ],
        4 * 10**9,
        2 * 10**7,
    )(place, *gathered, *tokens, out, low_back, du)
    up, summed = lax.optimization_barrier((up, summed))

    summed = summed.astype(F32).sum(0).astype(BF16)
    summed = jnp.broadcast_to(summed.reshape(4, 1, 24, 128), (4, 4, 24, 128)).reshape(16, 24, 128)
    summed = exchange(summed, ("zh", "zl"))

    here, there = call(
        backward,
        (shape((ROWS, WIDE)), shape((ROWS, WIDE))),
        [SM] + [HBM] * 7,
        (HBM, HBM),
        [
            pltpu.VMEM((BOTH, COT), BF16),
            pltpu.VMEM((HEADS, BOTH, BOTH), F32),
            pltpu.VMEM((BOTH, FEATURES), BF16),
            pltpu.VMEM((BOTH, WIDE), BF16),
            pltpu.SemaphoreType.DMA((14,)),
            pltpu.SemaphoreType.DMA((24,)),
            pltpu.SemaphoreType.DMA((26,)),
        ],
        4 * 10**9,
        2 * 10**7,
    )(place, *tokens, probs, up, blended)
    there, summed = lax.optimization_barrier((there, summed))

    other = permute(there, other_core)
    back = call(
        choose, shape((ROWS, WIDE)), [SM, HBM, HBM], VM, [pltpu.SemaphoreType.DMA((1,))], 10**6, 3 * 10**6
    )(place, here, other)
    back = exchange(back.reshape(16, 8, WIDE), ("y", "zl")).reshape(ROWS, WIDE)

    summed = summed.astype(F32).sum(0).astype(BF16)
    summed = lax.all_gather(summed, "y", tiled=True)
    pair = permute(summed, other_core)
    summed = jnp.stack([jnp.where(c == 0, pair, summed), jnp.where(c == 0, summed, pair)]).astype(F32)
    grad_up = jnp.swapaxes(summed[:, :, :RANK], 1, 2)
    grad_down = summed[:, :, RANK:]

    mine = jnp.where(c == 0, other, here)
    total = [
        (mine[:, at : at + FEATURES].astype(F32) + back[:, at : at + FEATURES].astype(F32)).astype(BF16).reshape(out_dims)
        for at in (COT, 0, FEATURES, 2 * FEATURES)
    ]
    return (*total, grad_down, grad_up)


def solution(mesh):
    fine = Mesh(mesh.devices.reshape(SIZES), AXES)
    dp, seq = ("x", "zh"), ("y", "zl", "c")
    tokens = P(dp, seq, None, None)
    rows, columns = P(None, dp, None), P(None, None, dp)
    return jax.shard_map(
        local,
        mesh=fine,
        in_specs=(tokens,) * 4 + (rows, rows, columns),
        out_specs=(tokens,) * 4 + (rows, columns),
        check_vma=False,
    )
```

```python
import jax
import jax.numpy as jnp
from jax import lax
from jax.experimental import pallas as pl
from jax.experimental.pallas import tpu as pltpu
from jax.sharding import Mesh
from jax.sharding import PartitionSpec as P

HDIM = 128
HEADS = 12
FEATURES = 1536
ROWS = 128
BOTH = 2 * ROWS
RANK = 64
GAIN = 2.0
SCALE = HDIM ** (-0.5)
WIDE = 4 * FEATURES
COT = 3 * FEATURES
SLICE = 384
BLOCK = 256

AXES = ("x", "zh", "y", "zl", "c")
SIZES = (4, 4, 4, 4, 2)
F32 = jnp.float32
BF16 = jnp.bfloat16

VM = pl.BlockSpec(memory_space=pltpu.VMEM)
HBM = pl.BlockSpec(memory_space=pltpu.HBM)
SM = pl.BlockSpec(memory_space=pltpu.SMEM)


def nn(a, b):
    return lax.dot_general(a, b, (((1,), (0,)), ((), ())), preferred_element_type=F32)


def nt(a, b):
    return lax.dot_general(a, b, (((1,), (1,)), ((), ())), preferred_element_type=F32)


def tn(a, b):
    return lax.dot_general(a, b, (((0,), (0,)), ((), ())), preferred_element_type=F32)


def shape(dims, dtype=BF16):
    return jax.ShapeDtypeStruct(dims, dtype)


def call(kernel, out_shape, in_specs, out_specs, scratch, flops, nbytes, vmem_mib=62):
    return pl.pallas_call(
        kernel,
        out_shape=out_shape,
        in_specs=in_specs,
        out_specs=out_specs,
        scratch_shapes=scratch,
        compiler_params=pltpu.CompilerParams(vmem_limit_bytes=vmem_mib * 2**20),
        cost_estimate=pl.CostEstimate(flops=flops, bytes_accessed=nbytes, transcendentals=0),
    )


def head(ref, h, base=0):
    return ref[:, base + h * HDIM : base + (h + 1) * HDIM]


def piece_of(arrays, second, first):
    return arrays[second][first // 2].at[first % 2]


def wait_all(copies):
    for copy in copies:
        copy.wait()


def start_rows(place, time, space, other_time, other_space, rows, sems, spans):
    def copies(own, other):
        return [
            (
                pltpu.make_async_copy(own.at[:, at:to], rows.at[0:ROWS, into : into + to - at], sems.at[2 * i]),
                pltpu.make_async_copy(other.at[:, at:to], rows.at[ROWS:BOTH, into : into + to - at], sems.at[2 * i + 1]),
            )
            for i, (at, to, into) in enumerate(spans)
        ]

    @pl.when(place[3] == 0)
    def _():
        for pair in copies(time, other_time):
            wait_none(pair)

    @pl.when(place[3] != 0)
    def _():
        for pair in copies(space, other_space):
            wait_none(pair)

    return copies(time, other_time)


def wait_none(copies):
    for copy in copies:
        copy.start()


def forward(
    place, e0, l0, e1, l1, e2, l2, e3, l3, time, space, other_time, other_space,
    probs_out, out_out, du_out, low_back_out, grads_out, rows, probs, out, du, low_back, grads, sems, row_sems, du_sems,
):
    arrays = ((e0, l0), (e1, l1), (e2, l2), (e3, l3))
    x, y, c = place[0], place[1], place[3]

    def pieces(first_is_x):
        made = []
        for across in range(4):
            for steps in (0, 2):
                second, first = (steps, across) if first_is_x else (across, steps)
                half = ((y - steps) & 3) >> 1
                for part in range(3):
                    made.append(
                        pltpu.make_async_copy(
                            piece_of(arrays, second, first).at[:, 96:112, part * 128 : part * 128 + 128],
                            du.at[pl.ds(((x - across) & 3) * 4, 4), pl.ds(pl.multiple_of(48 * half + 16 * part, 16), 16)],
                            du_sems.at[len(made)],
                        )
                    )
        return made

    loads = start_rows(place, time, space, other_time, other_space, rows, row_sems, [(0, WIDE, 0)])

    @pl.when(c == 0)
    def _():
        wait_none(pieces(True))

    @pl.when(c != 0)
    def _():
        wait_none(pieces(False))

    across = lax.broadcasted_iota(jnp.int32, (BOTH, BOTH), 0)
    along = lax.broadcasted_iota(jnp.int32, (BOTH, BOTH), 1)
    mask = jnp.where(c == 0, across & 7, across >> 7) == jnp.where(c == 0, along & 7, along >> 7)
    wait_all(loads[0])
    for h in range(HEADS):
        scores = nt(head(rows, h), head(rows, h, FEATURES)) * SCALE
        scores = jnp.where(mask, scores, -1e30)
        scores = jnp.exp(scores - jnp.max(scores, axis=-1, keepdims=True))
        value = (scores / jnp.sum(scores, axis=-1, keepdims=True)).astype(BF16)
        probs[h] = value
        out[:, h * HDIM : (h + 1) * HDIM] = nn(value, head(rows, h, 2 * FEATURES)).astype(BF16)
    wait_all(pieces(True))
    copies = [
        pltpu.make_async_copy(probs, probs_out, sems.at[0]),
        pltpu.make_async_copy(out, out_out, sems.at[1]),
        pltpu.make_async_copy(du, du_out, sems.at[2]),
    ]
    wait_none(copies)
    factors = du[...].reshape(FEATURES, 128)
    left = lax.broadcasted_iota(jnp.int32, (BOTH, 128), 1) < RANK
    low_back[...] = jnp.where(left, nn(out[...], factors), nn(rows[:, COT:], factors)).astype(BF16)
    left = lax.broadcasted_iota(jnp.int32, (FEATURES, 128), 1) < RANK
    total = GAIN * jnp.where(left, tn(rows[:, COT:], low_back[...]), tn(out[...], low_back[...]))
    total = [
        total[((x_at * 4 + zh_at) * 4 + y_at) * 24 :][:24] for x_at in range(4) for y_at in range(4) for zh_at in range(4)
    ]
    grads[...] = jnp.concatenate(total, axis=0).astype(BF16)
    copies += [
        pltpu.make_async_copy(low_back, low_back_out, sems.at[3]),
        pltpu.make_async_copy(grads, grads_out, sems.at[4]),
    ]
    wait_none(copies[-2:])
    wait_all(copies)


def project(
    place, e0, l0, e1, l1, e2, l2, e3, l3, time, space, other_time, other_space, out_in, low_back_in, du_in,
    up_out, blended_out, weight, rows, out, low_back, du, up, blended, sems, row_sems, weight_sems,
):
    x, y, c = place[0], place[1], place[3]
    copies = []
    for second in range(4):
        for first in range(4):
            row = jnp.where(c == 0, x - first, x - second) & 3
            column = jnp.where(c == 0, y - second, y - first) & 3
            copies.append(
                pltpu.make_async_copy(
                    piece_of(((e0, l0), (e1, l1), (e2, l2), (e3, l3)), second, first).at[:, 0:96, :],
                    weight.at[pl.ds(row * 4, 4), :, pl.ds(pl.multiple_of(column * SLICE, 128), SLICE)],
                    weight_sems.at[len(copies)],
                )
            )
            copies[-1].start()
    smaller = [
        pltpu.make_async_copy(source, target, sems.at[i])
        for i, (source, target) in enumerate(((out_in, out), (low_back_in, low_back), (du_in, du)))
    ]
    wait_none(smaller)
    loads = start_rows(place, time, space, other_time, other_space, rows, row_sems, [(COT, WIDE, 0)])
    wait_all(copies + smaller)
    wait_all(loads[0])
    whole = weight.reshape(FEATURES, FEATURES)
    factors_of = du.reshape(FEATURES, 128)
    zero = jnp.zeros((), BF16)

    def step(i, _):
        at = pl.multiple_of(i * BLOCK, BLOCK)
        factors = factors_of[pl.ds(at, BLOCK), :]
        is_down = lax.broadcasted_iota(jnp.int32, (BLOCK, 128), 1) < RANK
        down = jnp.where(is_down, factors, zero)
        upper = jnp.where(is_down, zero, factors)
        swapped = jnp.concatenate([low_back[:, RANK:], low_back[:, :RANK]], axis=1)
        upstream = nt(rows[...], whole[pl.ds(at, BLOCK), :]) + GAIN * nt(swapped, down)
        up[:, pl.ds(at, BLOCK)] = upstream.astype(BF16)
        total = nn(out[...], whole[:, pl.ds(at, BLOCK)]) + GAIN * nt(swapped, upper)
        blended[:, pl.ds(at, BLOCK)] = total.astype(BF16)
        return 0

    lax.fori_loop(0, FEATURES // BLOCK, step, 0)
    copies = [
        pltpu.make_async_copy(up, up_out, sems.at[3]),
        pltpu.make_async_copy(blended, blended_out, sems.at[4]),
    ]
    wait_none(copies)
    wait_all(copies)


def backward(
    place, time, space, other_time, other_space, probs_in, up_in, blended_in,
    here_out, there_out, rows, probs, up, sent, sems, row_sems,
):
    loads = [
        pltpu.make_async_copy(up_in, up, sems.at[0]),
        pltpu.make_async_copy(probs_in, probs, sems.at[1]),
        pltpu.make_async_copy(blended_in, sent.at[:, COT:], sems.at[2]),
    ]
    wait_none(loads)
    load_rows = start_rows(place, time, space, other_time, other_space, rows, row_sems, [(0, COT, 0)])
    wait_all(loads)
    wait_all(load_rows[0])
    for h in range(HEADS):
        value = probs[h]
        upstream = head(up, h)
        value_term = tn(value, upstream)
        value = value.astype(F32)
        prob_term = nt(upstream, head(rows, h, 2 * FEATURES))
        centre = jnp.sum(value * prob_term, axis=-1, keepdims=True)
        score_term = (value * (prob_term - centre) * SCALE).astype(BF16)
        terms = (nn(score_term, head(rows, h, FEATURES)), tn(score_term, head(rows, h)), value_term)
        for i, term in enumerate(terms):
            at = i * FEATURES + h * HDIM
            sent[:, at : at + HDIM] = term.astype(BF16)
    copies = [
        pltpu.make_async_copy(sent.at[0:ROWS], here_out, sems.at[3]),
        pltpu.make_async_copy(sent.at[ROWS:BOTH], there_out, sems.at[4]),
    ]
    wait_none(copies)
    wait_all(copies)


def choose(place, on_first, on_second, out, held, sems):
    parts = [pl.ds(at, FEATURES) for at in range(0, WIDE, FEATURES)]

    def loads(source):
        return [pltpu.make_async_copy(source.at[:, at], held.at[:, at], sems.at[i]) for i, at in enumerate(parts)]

    @pl.when(place[3] == 0)
    def _():
        wait_none(loads(on_first))

    @pl.when(place[3] != 0)
    def _():
        wait_none(loads(on_second))

    stores = [pltpu.make_async_copy(held.at[:, at], out.at[:, at], sems.at[4 + i]) for i, at in enumerate(parts)]
    for load, store in zip(loads(on_first), stores):
        load.wait()
        store.start()
    wait_all(stores)


def index_of(x, zh, y, zl, c):
    return (((x * 4 + zh) * 4 + y) * 4 + zl) * 2 + c


def permute(value, move):
    pairs = []
    for x in range(4):
        for zh in range(4):
            for y in range(4):
                for zl in range(4):
                    for c in range(2):
                        to = move(x, zh, y, zl, c)
                        if to is not None:
                            pairs.append((index_of(x, zh, y, zl, c), index_of(*to)))
    return lax.ppermute(value, AXES, pairs)


def along_first(step):
    return lambda x, zh, y, zl, c: ((x + step) % 4, zh, y, zl, c) if c == 0 else (x, zh, (y + step) % 4, zl, c)


def along_second(step):
    return lambda x, zh, y, zl, c: (x, zh, (y + step) % 4, zl, c) if c == 0 else ((x + step) % 4, zh, y, zl, c)


def other_core(x, zh, y, zl, c):
    return (x, zh, y, zl, 1 - c)


def to_first_core(x, zh, y, zl, c):
    return (x, zh, y, zl, 0) if c == 1 else None


def to_second_core(x, zh, y, zl, c):
    return (x, zh, y, zl, 1) if c == 0 else None


def exchange(value, axes):
    return lax.all_to_all(value, axes, split_axis=0, concat_axis=0, tiled=True)


def local(q, k, v, cot, weight, down, up):
    out_dims = q.shape
    x, zh, y, c = (lax.axis_index(n) for n in ("x", "zh", "y", "c"))
    place = jnp.stack([x, y, zh, c]).astype(jnp.int32)
    space = jnp.concatenate([a.reshape(ROWS, FEATURES) for a in (q, k, v, cot)], axis=1)

    branch = 1 - c
    piece = lax.dynamic_slice(weight, (branch, 0, y * SLICE), (1, 96, SLICE))[0]
    adapters = jnp.concatenate([down, jnp.swapaxes(up, 1, 2)], axis=2)
    adapters = lax.dynamic_slice(adapters, (branch, (y // 2) * 48, 0), (1, 48, 128))
    adapters = adapters.reshape(3, 16, 128).transpose(1, 0, 2).reshape(16, SLICE)
    first = jnp.concatenate([piece, adapters], axis=0)
    held = lax.all_gather(first, "zh")

    other_space = permute(space, to_second_core)
    space, held = lax.optimization_barrier((space, held))
    arrived = [permute(held, along_first(s)) for s in (1, 2, 3)]
    time = exchange(space.reshape(16, 8, WIDE), ("y", "zl")).reshape(ROWS, WIDE)
    early, late = jnp.stack([held, arrived[0]]), jnp.stack(arrived[1:])
    early_below, late_above = permute(early, along_second(1)), permute(late, along_second(3))
    early_above, late_below = permute(early, along_second(3)), permute(late, along_second(1))
    early_far, late_far = permute(early_below, along_second(1)), permute(late_above, along_second(3))
    gathered = [early, late, early_below, late_below, early_far, late_far, early_above, late_above]
    time, other_space, *gathered = lax.optimization_barrier((time, other_space, *gathered))
    other_time = permute(time, to_first_core)
    tokens = (time, space, other_time, other_space)

    probs, out, du, low_back, grads = call(
        forward,
        (
            shape((HEADS, BOTH, BOTH)),
            shape((BOTH, FEATURES)),
            shape((16, 96, 128)),
            shape((BOTH, 128)),
            shape((FEATURES, 128)),
        ),
        [SM] + [HBM] * 12,
        (HBM,) * 5,
        [
            pltpu.VMEM((BOTH, WIDE), BF16),
            pltpu.VMEM((HEADS, BOTH, BOTH), BF16),
            pltpu.VMEM((BOTH, FEATURES), BF16),
            pltpu.VMEM((16, 96, 128), BF16),
            pltpu.VMEM((BOTH, 128), BF16),
            pltpu.VMEM((FEATURES, 128), BF16),
            pltpu.SemaphoreType.DMA((5,)),
            pltpu.SemaphoreType.DMA((2,)),
            pltpu.SemaphoreType.DMA((24,)),
        ],
        8 * 10**8,
        10**7,
    )(place, *gathered, *tokens)

    summed = grads.reshape(16, 96, 128)
    summed = exchange(summed, ("x", "y"))

    up, blended = call(
        project,
        (shape((BOTH, FEATURES)), shape((BOTH, FEATURES))),
        [SM] + [HBM] * 15,
        (HBM, HBM),
        [
            pltpu.VMEM((16, 96, FEATURES), BF16),
            pltpu.VMEM((BOTH, FEATURES), BF16),
            pltpu.VMEM((BOTH, FEATURES), BF16),
            pltpu.VMEM((BOTH, 128), BF16),
            pltpu.VMEM((16, 96, 128), BF16),
            pltpu.VMEM((BOTH, FEATURES), BF16),
            pltpu.VMEM((BOTH, FEATURES), BF16),
            pltpu.SemaphoreType.DMA((5,)),
            pltpu.SemaphoreType.DMA((2,)),
            pltpu.SemaphoreType.DMA((16,)),
        ],
        4 * 10**9,
        2 * 10**7,
    )(place, *gathered, *tokens, out, low_back, du)
    up, summed = lax.optimization_barrier((up, summed))

    summed = summed.astype(F32).sum(0).astype(BF16)
    summed = jnp.broadcast_to(summed.reshape(4, 1, 24, 128), (4, 4, 24, 128)).reshape(16, 24, 128)
    summed = exchange(summed, ("zh", "zl"))

    here, there = call(
        backward,
        (shape((ROWS, WIDE)), shape((ROWS, WIDE))),
        [SM] + [HBM] * 7,
        (HBM, HBM),
        [
            pltpu.VMEM((BOTH, COT), BF16),
            pltpu.VMEM((HEADS, BOTH, BOTH), BF16),
            pltpu.VMEM((BOTH, FEATURES), BF16),
            pltpu.VMEM((BOTH, WIDE), BF16),
            pltpu.SemaphoreType.DMA((5,)),
            pltpu.SemaphoreType.DMA((2,)),
        ],
        4 * 10**9,
        2 * 10**7,
    )(place, *tokens, probs, up, blended)
    there, summed = lax.optimization_barrier((there, summed))

    other = permute(there, other_core)
    back = call(
        choose, shape((ROWS, WIDE)), [SM, HBM, HBM], HBM, [pltpu.VMEM((ROWS, WIDE), BF16), pltpu.SemaphoreType.DMA((8,))], 10**6, 3 * 10**6
    )(place, here, other)
    back = exchange(back.reshape(16, 8, WIDE), ("y", "zl")).reshape(ROWS, WIDE)

    summed = summed.astype(F32).sum(0).astype(BF16)
    summed = lax.all_gather(summed, "y", tiled=True)
    pair = permute(summed, other_core)
    summed = jnp.stack([jnp.where(c == 0, pair, summed), jnp.where(c == 0, summed, pair)]).astype(F32)
    grad_up = jnp.swapaxes(summed[:, :, :RANK], 1, 2)
    grad_down = summed[:, :, RANK:]

    mine = jnp.where(c == 0, other, here)
    total = [
        (mine[:, at : at + FEATURES].astype(F32) + back[:, at : at + FEATURES].astype(F32)).astype(BF16).reshape(out_dims)
        for at in (COT, 0, FEATURES, 2 * FEATURES)
    ]
    return (*total, grad_down, grad_up)


def solution(mesh):
    fine = Mesh(mesh.devices.reshape(SIZES), AXES)
    dp, seq = ("x", "zh"), ("y", "zl", "c")
    tokens = P(dp, seq, None, None)
    rows, columns = P(None, dp, None), P(None, None, dp)
    return jax.shard_map(
        local,
        mesh=fine,
        in_specs=(tokens,) * 4 + (rows, rows, columns),
        out_specs=(tokens,) * 4 + (rows, columns),
        check_vma=False,
    )
```

```python
import jax
import jax.numpy as jnp
from jax import lax
from jax.experimental import pallas as pl
from jax.experimental.pallas import tpu as pltpu
from jax.sharding import Mesh
from jax.sharding import PartitionSpec as P

HDIM = 128
HEADS = 12
FEATURES = 1536
ROWS = 128
BOTH = 2 * ROWS
RANK = 64
GAIN = 2.0
SCALE = HDIM ** (-0.5)
WIDE = 4 * FEATURES
COT = 3 * FEATURES
SLICE = 384
BLOCK = 256

AXES = ("x", "zh", "y", "zl", "c")
SIZES = (4, 4, 4, 4, 2)
F32 = jnp.float32
BF16 = jnp.bfloat16

VM = pl.BlockSpec(memory_space=pltpu.VMEM)
HBM = pl.BlockSpec(memory_space=pltpu.HBM)
SM = pl.BlockSpec(memory_space=pltpu.SMEM)


def nn(a, b):
    return lax.dot_general(a, b, (((1,), (0,)), ((), ())), preferred_element_type=F32)


def nt(a, b):
    return lax.dot_general(a, b, (((1,), (1,)), ((), ())), preferred_element_type=F32)


def tn(a, b):
    return lax.dot_general(a, b, (((0,), (0,)), ((), ())), preferred_element_type=F32)


def shape(dims, dtype=BF16):
    return jax.ShapeDtypeStruct(dims, dtype)


def call(kernel, out_shape, in_specs, out_specs, scratch, flops, nbytes, vmem_mib=62):
    return pl.pallas_call(
        kernel,
        out_shape=out_shape,
        in_specs=in_specs,
        out_specs=out_specs,
        scratch_shapes=scratch,
        compiler_params=pltpu.CompilerParams(vmem_limit_bytes=vmem_mib * 2**20),
        cost_estimate=pl.CostEstimate(flops=flops, bytes_accessed=nbytes, transcendentals=0),
    )


def head(ref, h, base=0):
    return ref[:, base + h * HDIM : base + (h + 1) * HDIM]


def piece_of(arrays, second, first):
    return arrays[second][first // 2].at[first % 2]


def wait_all(copies):
    for copy in copies:
        copy.wait()


def start_rows(place, time, space, other_time, other_space, rows, sems, spans):
    def copies(own, other):
        return [
            (
                pltpu.make_async_copy(own.at[:, at:to], rows.at[0:ROWS, into : into + to - at], sems.at[2 * i]),
                pltpu.make_async_copy(other.at[:, at:to], rows.at[ROWS:BOTH, into : into + to - at], sems.at[2 * i + 1]),
            )
            for i, (at, to, into) in enumerate(spans)
        ]

    @pl.when(place[3] == 0)
    def _():
        for pair in copies(time, other_time):
            wait_none(pair)

    @pl.when(place[3] != 0)
    def _():
        for pair in copies(space, other_space):
            wait_none(pair)

    return copies(time, other_time)


def wait_none(copies):
    for copy in copies:
        copy.start()


def forward(
    place, e0, l0, e1, l1, e2, l2, e3, l3, time, space, other_time, other_space,
    probs_out, out_out, du_out, low_back_out, grads_out, rows, probs, out, du, low_back, grads, sems, row_sems, du_sems,
):
    arrays = ((e0, l0), (e1, l1), (e2, l2), (e3, l3))
    x, y, c = place[0], place[1], place[3]

    def pieces(first_is_x):
        made = []
        for across in range(4):
            for steps in (0, 2):
                second, first = (steps, across) if first_is_x else (across, steps)
                half = ((y - steps) & 3) >> 1
                for part in range(3):
                    made.append(
                        pltpu.make_async_copy(
                            piece_of(arrays, second, first).at[:, 96:112, part * 128 : part * 128 + 128],
                            du.at[pl.ds(((x - across) & 3) * 4, 4), pl.ds(pl.multiple_of(48 * half + 16 * part, 16), 16)],
                            du_sems.at[len(made)],
                        )
                    )
        return made

    loads = start_rows(place, time, space, other_time, other_space, rows, row_sems, [(0, WIDE, 0)])

    @pl.when(c == 0)
    def _():
        wait_none(pieces(True))

    @pl.when(c != 0)
    def _():
        wait_none(pieces(False))

    across = lax.broadcasted_iota(jnp.int32, (BOTH, BOTH), 0)
    along = lax.broadcasted_iota(jnp.int32, (BOTH, BOTH), 1)
    mask = jnp.where(c == 0, across & 7, across >> 7) == jnp.where(c == 0, along & 7, along >> 7)
    wait_all(loads[0])
    for h in range(HEADS):
        scores = nt(head(rows, h), head(rows, h, FEATURES)) * SCALE
        scores = jnp.where(mask, scores, -1e30)
        scores = jnp.exp(scores - jnp.max(scores, axis=-1, keepdims=True))
        value = (scores / jnp.sum(scores, axis=-1, keepdims=True)).astype(BF16)
        probs[h] = value
        out[:, h * HDIM : (h + 1) * HDIM] = nn(value, head(rows, h, 2 * FEATURES)).astype(BF16)
    wait_all(pieces(True))
    copies = [
        pltpu.make_async_copy(probs, probs_out, sems.at[0]),
        pltpu.make_async_copy(out, out_out, sems.at[1]),
        pltpu.make_async_copy(du, du_out, sems.at[2]),
    ]
    wait_none(copies)
    factors = du[...].reshape(FEATURES, 128)
    left = lax.broadcasted_iota(jnp.int32, (BOTH, 128), 1) < RANK
    low_back[...] = jnp.where(left, nn(out[...], factors), nn(rows[:, COT:], factors)).astype(BF16)
    left = lax.broadcasted_iota(jnp.int32, (FEATURES, 128), 1) < RANK
    total = GAIN * jnp.where(left, tn(rows[:, COT:], low_back[...]), tn(out[...], low_back[...]))
    total = [
        total[((x_at * 4 + zh_at) * 4 + y_at) * 24 :][:24] for x_at in range(4) for y_at in range(4) for zh_at in range(4)
    ]
    grads[...] = jnp.concatenate(total, axis=0).astype(BF16)
    copies += [
        pltpu.make_async_copy(low_back, low_back_out, sems.at[3]),
        pltpu.make_async_copy(grads, grads_out, sems.at[4]),
    ]
    wait_none(copies[-2:])
    wait_all(copies)


def project(
    place, e0, l0, e1, l1, e2, l2, e3, l3, time, space, other_time, other_space, out_in, low_back_in, du_in,
    up_out, blended_out, weight, rows, out, low_back, du, up, blended, sems, row_sems, weight_sems,
):
    x, y, c = place[0], place[1], place[3]
    copies = []
    for second in range(4):
        for first in range(4):
            row = jnp.where(c == 0, x - first, x - second) & 3
            column = jnp.where(c == 0, y - second, y - first) & 3
            copies.append(
                pltpu.make_async_copy(
                    piece_of(((e0, l0), (e1, l1), (e2, l2), (e3, l3)), second, first).at[:, 0:96, :],
                    weight.at[pl.ds(row * 4, 4), :, pl.ds(pl.multiple_of(column * SLICE, 128), SLICE)],
                    weight_sems.at[len(copies)],
                )
            )
            copies[-1].start()
    smaller = [
        pltpu.make_async_copy(source, target, sems.at[i])
        for i, (source, target) in enumerate(((out_in, out), (low_back_in, low_back), (du_in, du)))
    ]
    wait_none(smaller)
    loads = start_rows(place, time, space, other_time, other_space, rows, row_sems, [(COT, WIDE, 0)])
    wait_all(copies + smaller)
    wait_all(loads[0])
    whole = weight.reshape(FEATURES, FEATURES)
    factors_of = du.reshape(FEATURES, 128)
    zero = jnp.zeros((), BF16)

    def step(i, _):
        at = pl.multiple_of(i * BLOCK, BLOCK)
        factors = factors_of[pl.ds(at, BLOCK), :]
        is_down = lax.broadcasted_iota(jnp.int32, (BLOCK, 128), 1) < RANK
        down = jnp.where(is_down, factors, zero)
        upper = jnp.where(is_down, zero, factors)
        swapped = jnp.concatenate([low_back[:, RANK:], low_back[:, :RANK]], axis=1)
        upstream = nt(rows[...], whole[pl.ds(at, BLOCK), :]) + GAIN * nt(swapped, down)
        up[:, pl.ds(at, BLOCK)] = upstream.astype(BF16)
        total = nn(out[...], whole[:, pl.ds(at, BLOCK)]) + GAIN * nt(swapped, upper)
        blended[:, pl.ds(at, BLOCK)] = total.astype(BF16)
        return 0

    lax.fori_loop(0, FEATURES // BLOCK, step, 0)
    copies = [
        pltpu.make_async_copy(up, up_out, sems.at[3]),
        pltpu.make_async_copy(blended, blended_out, sems.at[4]),
    ]
    wait_none(copies)
    wait_all(copies)


def backward(
    place, time, space, other_time, other_space, probs_in, up_in, blended_in,
    here_out, there_out, rows, probs, up, sent, sems, row_sems,
):
    loads = [
        pltpu.make_async_copy(up_in, up, sems.at[0]),
        pltpu.make_async_copy(probs_in, probs, sems.at[1]),
        pltpu.make_async_copy(blended_in, sent.at[:, COT:], sems.at[2]),
    ]
    wait_none(loads)
    load_rows = start_rows(place, time, space, other_time, other_space, rows, row_sems, [(0, COT, 0)])
    wait_all(loads)
    wait_all(load_rows[0])
    for h in range(HEADS):
        value = probs[h]
        upstream = head(up, h)
        value_term = tn(value, upstream)
        value = value.astype(F32)
        prob_term = nt(upstream, head(rows, h, 2 * FEATURES))
        centre = jnp.sum(value * prob_term, axis=-1, keepdims=True)
        score_term = (value * (prob_term - centre) * SCALE).astype(BF16)
        terms = (nn(score_term, head(rows, h, FEATURES)), tn(score_term, head(rows, h)), value_term)
        for i, term in enumerate(terms):
            at = i * FEATURES + h * HDIM
            sent[:, at : at + HDIM] = term.astype(BF16)
    copies = [
        pltpu.make_async_copy(sent.at[0:ROWS], here_out, sems.at[3]),
        pltpu.make_async_copy(sent.at[ROWS:BOTH], there_out, sems.at[4]),
    ]
    wait_none(copies)
    wait_all(copies)


def choose(place, on_first, on_second, out, held, sems):
    parts = [pl.ds(at, FEATURES) for at in range(0, WIDE, FEATURES)]

    def loads(source):
        return [pltpu.make_async_copy(source.at[:, at], held.at[:, at], sems.at[i]) for i, at in enumerate(parts)]

    @pl.when(place[3] == 0)
    def _():
        wait_none(loads(on_first))

    @pl.when(place[3] != 0)
    def _():
        wait_none(loads(on_second))

    stores = [pltpu.make_async_copy(held.at[:, at], out.at[:, at], sems.at[4 + i]) for i, at in enumerate(parts)]
    for load, store in zip(loads(on_first), stores):
        load.wait()
        store.start()
    wait_all(stores)


def index_of(x, zh, y, zl, c):
    return (((x * 4 + zh) * 4 + y) * 4 + zl) * 2 + c


def permute(value, move):
    pairs = []
    for x in range(4):
        for zh in range(4):
            for y in range(4):
                for zl in range(4):
                    for c in range(2):
                        to = move(x, zh, y, zl, c)
                        if to is not None:
                            pairs.append((index_of(x, zh, y, zl, c), index_of(*to)))
    return lax.ppermute(value, AXES, pairs)


def along_first(step):
    return lambda x, zh, y, zl, c: ((x + step) % 4, zh, y, zl, c) if c == 0 else (x, zh, (y + step) % 4, zl, c)


def along_second(step):
    return lambda x, zh, y, zl, c: (x, zh, (y + step) % 4, zl, c) if c == 0 else ((x + step) % 4, zh, y, zl, c)


def other_core(x, zh, y, zl, c):
    return (x, zh, y, zl, 1 - c)


def to_first_core(x, zh, y, zl, c):
    return (x, zh, y, zl, 0) if c == 1 else None


def to_second_core(x, zh, y, zl, c):
    return (x, zh, y, zl, 1) if c == 0 else None


def exchange(value, axes):
    return lax.all_to_all(value, axes, split_axis=0, concat_axis=0, tiled=True)


def local(q, k, v, cot, weight, down, up):
    out_dims = q.shape
    x, zh, y, c = (lax.axis_index(n) for n in ("x", "zh", "y", "c"))
    place = jnp.stack([x, y, zh, c]).astype(jnp.int32)
    space = jnp.concatenate([a.reshape(ROWS, FEATURES) for a in (q, k, v, cot)], axis=1)

    branch = 1 - c
    piece = lax.dynamic_slice(weight, (branch, 0, y * SLICE), (1, 96, SLICE))[0]
    adapters = jnp.concatenate([down, jnp.swapaxes(up, 1, 2)], axis=2)
    adapters = lax.dynamic_slice(adapters, (branch, (y // 2) * 48, 0), (1, 48, 128))
    adapters = adapters.reshape(3, 16, 128).transpose(1, 0, 2).reshape(16, SLICE)
    first = jnp.concatenate([piece, adapters], axis=0)
    held = lax.all_gather(first, "zh")

    other_space = permute(space, to_second_core)
    space, held = lax.optimization_barrier((space, held))
    arrived = [permute(held, along_first(s)) for s in (1, 2, 3)]
    time = exchange(space.reshape(16, 8, WIDE), ("y", "zl")).reshape(ROWS, WIDE)
    early, late = jnp.stack([held, arrived[0]]), jnp.stack(arrived[1:])
    early_below, late_above = permute(early, along_second(1)), permute(late, along_second(3))
    early_above, late_below = permute(early, along_second(3)), permute(late, along_second(1))
    early_far, late_far = permute(early_below, along_second(1)), permute(late_above, along_second(3))
    gathered = [early, late, early_below, late_below, early_far, late_far, early_above, late_above]
    time, other_space, *gathered = lax.optimization_barrier((time, other_space, *gathered))
    other_time = permute(time, to_first_core)
    tokens = (time, space, other_time, other_space)

    probs, out, du, low_back, grads = call(
        forward,
        (
            shape((HEADS, BOTH, BOTH)),
            shape((BOTH, FEATURES)),
            shape((16, 96, 128)),
            shape((BOTH, 128)),
            shape((FEATURES, 128)),
        ),
        [SM] + [HBM] * 12,
        (HBM,) * 5,
        [
            pltpu.VMEM((BOTH, WIDE), BF16),
            pltpu.VMEM((HEADS, BOTH, BOTH), BF16),
            pltpu.VMEM((BOTH, FEATURES), BF16),
            pltpu.VMEM((16, 96, 128), BF16),
            pltpu.VMEM((BOTH, 128), BF16),
            pltpu.VMEM((FEATURES, 128), BF16),
            pltpu.SemaphoreType.DMA((5,)),
            pltpu.SemaphoreType.DMA((2,)),
            pltpu.SemaphoreType.DMA((24,)),
        ],
        8 * 10**8,
        10**7,
    )(place, *gathered, *tokens)

    summed = grads.reshape(16, 96, 128)
    summed = exchange(summed, ("x", "y"))

    up, blended = call(
        project,
        (shape((BOTH, FEATURES)), shape((BOTH, FEATURES))),
        [SM] + [HBM] * 15,
        (HBM, HBM),
        [
            pltpu.VMEM((16, 96, FEATURES), BF16),
            pltpu.VMEM((BOTH, FEATURES), BF16),
            pltpu.VMEM((BOTH, FEATURES), BF16),
            pltpu.VMEM((BOTH, 128), BF16),
            pltpu.VMEM((16, 96, 128), BF16),
            pltpu.VMEM((BOTH, FEATURES), BF16),
            pltpu.VMEM((BOTH, FEATURES), BF16),
            pltpu.SemaphoreType.DMA((5,)),
            pltpu.SemaphoreType.DMA((2,)),
            pltpu.SemaphoreType.DMA((16,)),
        ],
        4 * 10**9,
        2 * 10**7,
    )(place, *gathered, *tokens, out, low_back, du)
    up, summed = lax.optimization_barrier((up, summed))

    summed = summed.astype(F32).sum(0).astype(BF16)
    summed = jnp.broadcast_to(summed.reshape(4, 1, 24, 128), (4, 4, 24, 128)).reshape(16, 24, 128)
    summed = exchange(summed, ("zh", "zl"))

    here, there = call(
        backward,
        (shape((ROWS, WIDE)), shape((ROWS, WIDE))),
        [SM] + [HBM] * 7,
        (HBM, HBM),
        [
            pltpu.VMEM((BOTH, COT), BF16),
            pltpu.VMEM((HEADS, BOTH, BOTH), BF16),
            pltpu.VMEM((BOTH, FEATURES), BF16),
            pltpu.VMEM((BOTH, WIDE), BF16),
            pltpu.SemaphoreType.DMA((5,)),
            pltpu.SemaphoreType.DMA((2,)),
        ],
        4 * 10**9,
        2 * 10**7,
    )(place, *tokens, probs, up, blended)
    there, summed = lax.optimization_barrier((there, summed))

    other = permute(there, other_core)
    def by_core(on_first, on_second):
        return call(
            choose,
            shape((ROWS, WIDE)),
            [SM, HBM, HBM],
            HBM,
            [pltpu.VMEM((ROWS, WIDE), BF16), pltpu.SemaphoreType.DMA((8,))],
            10**6,
            3 * 10**6,
        )(place, on_first, on_second)

    back = by_core(here, other)
    back = exchange(back.reshape(16, 8, WIDE), ("y", "zl")).reshape(ROWS, WIDE)

    summed = summed.astype(F32).sum(0).astype(BF16)
    summed = lax.all_gather(summed, "y", tiled=True)
    here, other, summed = lax.optimization_barrier((here, other, summed))
    mine = by_core(other, here)
    pair = permute(summed, other_core)
    summed = jnp.stack([jnp.where(c == 0, pair, summed), jnp.where(c == 0, summed, pair)]).astype(F32)
    grad_up = jnp.swapaxes(summed[:, :, :RANK], 1, 2)
    grad_down = summed[:, :, RANK:]

    total = [
        (mine[:, at : at + FEATURES].astype(F32) + back[:, at : at + FEATURES].astype(F32)).astype(BF16).reshape(out_dims)
        for at in (COT, 0, FEATURES, 2 * FEATURES)
    ]
    return (*total, grad_down, grad_up)


def solution(mesh):
    fine = Mesh(mesh.devices.reshape(SIZES), AXES)
    dp, seq = ("x", "zh"), ("y", "zl", "c")
    tokens = P(dp, seq, None, None)
    rows, columns = P(None, dp, None), P(None, None, dp)
    return jax.shard_map(
        local,
        mesh=fine,
        in_specs=(tokens,) * 4 + (rows, rows, columns),
        out_specs=(tokens,) * 4 + (rows, columns),
        check_vma=False,
    )
```
